512 devices in a mesh: donor: 16 (over x, y_lo), gene: 32 (over z, y_hi, core).
Axes of the slice: x: 4, y: 8 (y_hi: 2, y_lo: 4; y = y_hi * 4 + y_lo), z: 8, core: 2. Of those that a mesh axis runs over, the one named last changes fastest.
Arguments:
- partition_tallies: bfloat16 [16384, 40352], P('donor', 'gene'), may hold values from 0 to 4
- blank_tallies: bfloat16 [4096, 40352], P('donor', 'gene'), may hold values from 0 to 1
- cluster_assignment: int32 [16384], P('donor'), may hold values from 0 to 63
- partition_person_label: int32 [16384], P('donor'), may hold values from 0 to 11
- person_blank_members: int32 [12, 384], replicated, may hold values from 0 to 4095
- spillover_fraction: float32 [16384], P('donor'), may hold values from 0.05 to 0.7
- cluster_expression: float32 [64, 40352], P(None, 'gene'), may hold values from 0.05 to 20
- background_profile: float32 [12, 40352], P(None, 'gene'), may hold values from 0.05 to 20
Outputs:
- new_profiles: float32 [64, 40352], P('donor', 'gene')
- new_ambient: float32 [12, 40352], P(None, 'gene')
- new_theta: float32 [16384], P('donor')
- ambient_reads: float32 [16384], P('donor')
The draws below stay inside these ranges and needn't reach their ends.
Inputs may be any that keep to these rules, and one draw needn't show every extreme that they name: `person_blank_members`: an index may be listed more than once.
All inputs are finite; a program needn't handle non-finite values.
Results may differ from the reference program's by a relative error of at most 0.0003.
Values sent between devices are 32-bit elements; how exact they have to be, the bound alone decides.
A program may use at most 64 MiB of HBM per device.

```python
import math
import jax
import jax.numpy as jnp
from jax import lax

TRANSCRIPT_TOTAL = 40352
POPS = 64
DONOR_NUMBER = 12
CELL_DEV = 1024
LIST_ENTRIES = 384
CELLS = 16384
BLANK_PARTITIONS = 4096
N_DONOR = 16


def touch_ends(entries, rng, smallest, top_value):
    longest = entries.shape.index(max(entries.shape))
    spots = []
    for shift in (0, 1):
        where = [jax.random.randint(jax.random.fold_in(rng, axis), (), 0, length) for axis, length in enumerate(entries.shape)]
        where[longest] = (where[longest] + shift) % entries.shape[longest]
        spots.append(tuple(where))
    return entries.at[spots[0]].set(smallest).at[spots[1]].set(top_value)


def level_of(stream_key, extent, shards, least, top_value):
    gain = 1.0
    for dim, parts in shards:
        heights = jax.random.uniform(jax.random.fold_in(jax.random.fold_in(stream_key, 6), dim), (parts,), jnp.float32, least / len(shards), top_value / len(shards))
        gain = gain * jnp.repeat(jnp.exp(heights), extent[dim] // parts).reshape((-1,) + (1,) * (len(extent) - 1 - dim))
    return gain


def setup_inputs(seed: int = 0) -> dict:
    arg_keys = jax.random.split(jax.random.key(seed), 9)
    return {
        "partition_tallies": jnp.clip(4.0 * jax.random.uniform(arg_keys[0], (CELLS, TRANSCRIPT_TOTAL), jnp.float32) ** level_of(arg_keys[0], (CELLS, TRANSCRIPT_TOTAL), ((0, 16), (1, 32)), -0.2, 0.2), 0.0, 4.0).astype(jnp.bfloat16),
        "blank_tallies": jnp.clip(1.0 * jax.random.uniform(arg_keys[1], (BLANK_PARTITIONS, TRANSCRIPT_TOTAL), jnp.float32) ** level_of(arg_keys[1], (BLANK_PARTITIONS, TRANSCRIPT_TOTAL), ((0, 16), (1, 32)), -0.2, 0.2), 0.0, 1.0).astype(jnp.bfloat16),
        "cluster_assignment": touch_ends(jax.random.randint(arg_keys[2], (CELLS,), 0, POPS), jax.random.fold_in(arg_keys[2], 1), 0, POPS - 1).astype(jnp.int32),
        "partition_person_label": touch_ends(jax.random.randint(arg_keys[3], (CELLS,), 0, DONOR_NUMBER), jax.random.fold_in(arg_keys[3], 1), 0, DONOR_NUMBER - 1).astype(jnp.int32),
        "person_blank_members": touch_ends(jax.random.randint(arg_keys[4], (DONOR_NUMBER, LIST_ENTRIES), 0, BLANK_PARTITIONS), jax.random.fold_in(arg_keys[4], 1), 0, BLANK_PARTITIONS - 1).astype(jnp.int32),
        "spillover_fraction": jnp.clip(0.05 + 0.65 * jax.random.uniform(arg_keys[5], (CELLS,), jnp.float32) ** level_of(arg_keys[5], (CELLS,), ((0, 16),), -0.2, 0.2), 0.05, 0.7),
        "cluster_expression": jnp.clip(jnp.exp(math.log(20.0) - 5.9914645 * jax.random.uniform(arg_keys[6], (POPS, TRANSCRIPT_TOTAL), jnp.float32) ** level_of(arg_keys[6], (POPS, TRANSCRIPT_TOTAL), ((1, 32),), -0.2, 0.2)), 0.05, 20.0),
        "background_profile": jnp.clip(jnp.exp(math.log(20.0) - 5.9914645 * jax.random.uniform(arg_keys[7], (DONOR_NUMBER, TRANSCRIPT_TOTAL), jnp.float32) ** level_of(arg_keys[7], (DONOR_NUMBER, TRANSCRIPT_TOTAL), ((1, 32),), -0.2, 0.2)), 0.05, 20.0),
    }


pseudo_count = 0.5
beta_prior = 10.0


def reference(partition_tallies, blank_tallies, cluster_assignment, partition_person_label, person_blank_members, spillover_fraction, cluster_expression, background_profile):
    def droplet_block(carry, pieces):
        pop_sums, background_transcript_totals = carry
        block_counts, block_labels, block_donors, block_theta = pieces
        weight_native = (1.0 - block_theta[:, None]) * cluster_expression[block_labels]
        weight_contam = block_theta[:, None] * background_profile[block_donors]
        resp_native = weight_native / (weight_native + weight_contam)
        count_values = block_counts.astype(jnp.float32)
        native = (count_values * resp_native).astype(jnp.bfloat16).astype(jnp.float32)
        contam = (count_values * (1.0 - resp_native)).astype(jnp.bfloat16).astype(jnp.float32)
        pop_hot = (block_labels[:, None] == jnp.arange(POPS, dtype=jnp.int32)[None, :]).astype(jnp.float32)
        donor_hot = (block_donors[:, None] == jnp.arange(DONOR_NUMBER, dtype=jnp.int32)[None, :]).astype(jnp.float32)
        pop_sums = pop_sums + jnp.dot(pop_hot.T, native, precision=lax.Precision.HIGHEST)
        background_transcript_totals = background_transcript_totals + jnp.dot(donor_hot.T, contam, precision=lax.Precision.HIGHEST)
        return (pop_sums, background_transcript_totals), (jnp.sum(native, axis=1), jnp.sum(contam, axis=1))

    start = (jnp.zeros((POPS, TRANSCRIPT_TOTAL), jnp.float32), jnp.zeros((DONOR_NUMBER, TRANSCRIPT_TOTAL), jnp.float32))
    pieces = (partition_tallies.reshape(N_DONOR, CELL_DEV, TRANSCRIPT_TOTAL), cluster_assignment.reshape(N_DONOR, CELL_DEV),
              partition_person_label.reshape(N_DONOR, CELL_DEV), spillover_fraction.reshape(N_DONOR, CELL_DEV))
    (pop_sums, background_transcript_totals), (native_reads, contam_reads) = lax.scan(droplet_block, start, pieces)
    native_reads = native_reads.reshape(CELLS)
    contam_reads = contam_reads.reshape(CELLS)
    gathered_blank_tallies = jnp.sum((person_blank_members[:, :, None] == jnp.arange(BLANK_PARTITIONS, dtype=jnp.int32)[None, None, :]).astype(jnp.float32), axis=1)
    background_transcript_totals = background_transcript_totals + jnp.dot(gathered_blank_tallies, blank_tallies.astype(jnp.float32), precision=lax.Precision.HIGHEST)
    new_profiles = TRANSCRIPT_TOTAL * (pop_sums + pseudo_count) / (jnp.sum(pop_sums, axis=1)[:, None] + TRANSCRIPT_TOTAL * pseudo_count)
    new_ambient = TRANSCRIPT_TOTAL * (background_transcript_totals + pseudo_count) / (jnp.sum(background_transcript_totals, axis=1)[:, None] + TRANSCRIPT_TOTAL * pseudo_count)
    new_theta = (contam_reads + beta_prior) / (native_reads + contam_reads + 2.0 * beta_prior)
    ambient_reads = contam_reads / TRANSCRIPT_TOTAL
    return new_profiles, new_ambient, new_theta, ambient_reads
```

```python
import jax
import jax.numpy as jnp
from jax import lax
from jax.experimental import pallas as pl
from jax.experimental.pallas import tpu as pltpu
from jax.sharding import PartitionSpec as P

TOTAL = 40352
PSEUDO = 0.5
BETA = 10.0
G, N, NB, GP = 1261, 1024, 256, 1280
POPS, DONORS = 64, 12
CHUNK = 256
EARLY = 24
ROWS = 48
f32, bf16 = jnp.float32, jnp.bfloat16
MESH = pl.DeviceIdType.MESH
LAST = (((1,), (1,)), ((), ()))
FIRST = (((0,), (0,)), ((), ()))


def thirds(v):
    hi = v.astype(bf16)
    rest = v - hi.astype(f32)
    mid = rest.astype(bf16)
    return hi, mid, (rest - mid.astype(f32)).astype(bf16)


def hot(mask):
    return jnp.where(mask, 1.0, 0.0).astype(bf16)


def padded_tail(ref):
    width = ref.shape[1]
    ragged = jnp.concatenate([ref[1248:G].astype(f32), jnp.zeros((3, width), f32)], axis=0)
    return jnp.concatenate([ref[1024:1248], ragged.astype(bf16), jnp.zeros((16, width), bf16)], axis=0)


def kernel(
    x_hbm, b_hbm, lab_hbm, don_hbm, mem_hbm, th_hbm, e_hbm, p_hbm,
    prof_ref, amb_ref, theta_ref, reads_ref,
    xs, bs, lab_v, don_v, mem_v, th_v, e_v, p_v, hots, table,
    send, got, mine, from_core, gene_out, gene_in, final_out, final_in, amb_all, tot_out, tot_in,
    in_sem, s_sem, r_sem,
):
    d = lax.axis_index("donor")
    q = lax.axis_index("gene")
    core = lax.rem(q, 2)
    other = {"gene": q + 1 - 2 * core}

    smalls = (
        (lab_hbm, lab_v), (don_hbm, don_v), (th_hbm, th_v), (e_hbm, e_v), (p_hbm, p_v), (mem_hbm, mem_v),
    )
    small_in = [pltpu.make_async_copy(a, b, in_sem.at[i]) for i, (a, b) in enumerate(smalls)]
    for c in small_in:
        c.start()
    x_in = []
    for c in range(5):
        rows = pl.ds(CHUNK * c, min(CHUNK, G - CHUNK * c))
        x_in.append(pltpu.make_async_copy(x_hbm.at[rows], xs.at[rows], in_sem.at[6 + c]))
    b_in = pltpu.make_async_copy(b_hbm, bs, in_sem.at[11])
    for c in x_in[:1] + [b_in] + x_in[1:]:
        c.start()

    barrier = pltpu.get_barrier_semaphore()

    def greet(j, carry):
        pl.semaphore_signal(barrier, inc=1, device_id={"donor": lax.rem(d + j, 16)}, device_id_type=MESH)
        pl.semaphore_signal(barrier, inc=1, device_id={"gene": lax.rem(q + 2 * j, 32)}, device_id_type=MESH)
        return carry

    lax.fori_loop(1, 16, greet, 0)
    pl.semaphore_signal(barrier, inc=1, device_id=other, device_id_type=MESH)

    for c in small_in:
        c.wait()
    labels, people, theta = lab_v[...], don_v[...], th_v[...]
    pop_hot = hot(labels == lax.broadcasted_iota(jnp.int32, (POPS, N), 0))
    donor_hot = hot(people == lax.broadcasted_iota(jnp.int32, (16, N), 0))
    for i in range(3):
        hots[64 * i : 64 * i + 64] = pop_hot
        hots[192 + 16 * i : 208 + 16 * i] = donor_hot
    row = lax.broadcasted_iota(jnp.int32, (16, N), 0)
    odds = jnp.zeros((16, N), f32)
    for i, v in enumerate(thirds((jnp.log(theta) - jnp.log(1.0 - theta)) * -0.5)):
        odds = jnp.where(row == i, v.astype(f32), odds)
    hots[240:256] = odds.astype(bf16)
    for i, v in enumerate(thirds(jnp.log(e_v[...]) * 0.5)):
        table[64 * i : 64 * i + 64, 0:G] = v
    log_ambient = jnp.concatenate([jnp.log(p_v[...]) * -0.5, jnp.zeros((4, G), f32)], axis=0)
    for i, v in enumerate(thirds(log_ambient)):
        table[192 + 16 * i : 208 + 16 * i, 0:G] = v
    table[240:256] = hot(lax.broadcasted_iota(jnp.int32, (16, GP), 0) < 3)
    table[0:240, G:GP] = jnp.zeros((240, GP - G), bf16)

    members = mem_v[...] - d * NB
    empties = lax.broadcasted_iota(jnp.int32, (NB, 128), 0)
    lane = lax.broadcasted_iota(jnp.int32, (128, 128), 1)
    listed = jnp.zeros((NB, 128), f32)
    for r in range(DONORS):
        count = jnp.zeros((NB, 128), f32)
        for t in range(3):
            count = count + jnp.where(members[r : r + 1, 128 * t : 128 * t + 128] == empties, 1.0, 0.0)
        listed = listed + jnp.dot(count.astype(bf16), hot(lane == POPS + r), preferred_element_type=f32)
    listed_hi = listed.astype(bf16)
    listed_lo = (listed - listed_hi.astype(f32)).astype(bf16)

    pops = jnp.concatenate([pop_hot, jnp.zeros((64, N), bf16)], axis=0)
    folk = jnp.concatenate([jnp.zeros((64, N), bf16), donor_hot, jnp.zeros((48, N), bf16)], axis=0)
    send[15, 40:48] = jnp.zeros((8, 128), f32)

    native_acc = jnp.zeros((8, N), f32)
    contam_acc = jnp.zeros((8, N), f32)
    totals = jnp.zeros((8, 128), f32)

    def spread(first, count, index):
        def one(j, carry):
            peer = lax.rem(d + j, 16)
            pltpu.make_async_remote_copy(
                send.at[peer, pl.ds(first, count)], got.at[j - 1, pl.ds(first, count)],
                s_sem.at[index], r_sem.at[index], device_id={"donor": peer}, device_id_type=MESH,
            ).start()
            return carry

        lax.fori_loop(1, 16, one, 0)

    for c in range(5):
        log_odds = lax.dot_general(table[:, CHUNK * c : CHUNK * c + CHUNK], hots[...], FIRST, preferred_element_type=f32)
        x_in[c].wait()
        if c == 0:
            b_in.wait()
        if c < 4:
            counts, blanks = xs[CHUNK * c : CHUNK * c + CHUNK], bs[CHUNK * c : CHUNK * c + CHUNK]
        else:
            counts, blanks = padded_tail(xs), padded_tail(bs)
        half = counts.astype(f32) * 0.5
        swing = half * jnp.tanh(log_odds)
        native = (half + swing).astype(bf16)
        contam = (half - swing).astype(bf16)
        native_acc = native_acc + jnp.sum(native.astype(f32).reshape(CHUNK // 8, 8, N), axis=0)
        contam_acc = contam_acc + jnp.sum(contam.astype(f32).reshape(CHUNK // 8, 8, N), axis=0)
        sums = lax.dot_general(native, pops, LAST, preferred_element_type=f32)
        sums = sums + lax.dot_general(contam, folk, LAST, preferred_element_type=f32)
        sums = sums + jnp.dot(blanks, listed_hi, preferred_element_type=f32)
        sums = sums + jnp.dot(blanks, listed_lo, preferred_element_type=f32)
        totals = totals + jnp.sum(sums.reshape(CHUNK // 8, 8, 128), axis=0)
        for h in range(2):
            t = 2 * c + h
            turned = sums[128 * h : 128 * h + 128].T
            for i in range(16):
                send[i, 4 * t : 4 * t + 4] = turned[4 * i : 4 * i + 4]
            r = 0
            while r < DONORS:
                u = 12 * t + r
                run = min(DONORS - r, 8 - u % 8)
                send[u // 8, 40 + u % 8 : 40 + u % 8 + run] = turned[64 + r : 64 + r + run]
                r += run
        if c == 2:
            pl.semaphore_wait(barrier, 31)
            spread(0, EARLY, 0)

    native_row = jnp.sum(native_acc, axis=0, keepdims=True)
    contam_row = jnp.sum(contam_acc, axis=0, keepdims=True)
    for i in range(8):
        mine[i : i + 1] = native_row[:, 128 * i : 128 * i + 128]
        mine[16 + i : 17 + i] = contam_row[:, 128 * i : 128 * i + 128]
    mine[8:16] = totals
    to_core = pltpu.make_async_remote_copy(
        mine.at[pl.ds(8 - 8 * core, 16)], from_core, s_sem.at[2], r_sem.at[2], device_id=other, device_id_type=MESH
    )
    to_core.start()
    spread(EARLY, ROWS - EARLY, 1)

    to_core.wait_recv()
    at_reads = pl.multiple_of(8 * core, 8)
    at_total = pl.multiple_of(8 - 8 * core, 8)
    gene_out[0:8] = mine[pl.ds(pl.multiple_of(16 * core, 8), 8)] + from_core[pl.ds(at_reads, 8)]
    gene_out[8:16] = mine[8:16] + from_core[pl.ds(at_total, 8)]

    def to_gene(j, carry):
        pltpu.make_async_remote_copy(
            gene_out, gene_in.at[j - 1], s_sem.at[3], r_sem.at[3],
            device_id={"gene": lax.rem(q + 2 * j, 32)}, device_id_type=MESH,
        ).start()
        return carry

    lax.fori_loop(1, 16, to_gene, 0)

    def wait_for(ref, sem):
        pltpu.make_async_copy(ref, ref, sem).wait()

    early, late = pl.ds(0, EARLY), pl.ds(EARLY, ROWS - EARLY)
    fifteen = pl.ds(0, 15)
    wait_for(got.at[fifteen, early], r_sem.at[0])
    wait_for(got.at[fifteen, late], r_sem.at[1])
    both = send[d] + jnp.sum(got[...], axis=0)
    amb_all[d] = both[40:48]

    def to_all(j, carry):
        pltpu.make_async_remote_copy(
            amb_all.at[d], amb_all.at[d], s_sem.at[4], r_sem.at[4],
            device_id={"donor": lax.rem(d + j, 16)}, device_id_type=MESH,
        ).start()
        return carry

    lax.fori_loop(1, 16, to_all, 0)

    wait_for(gene_in, r_sem.at[3])
    gene_sum = gene_out[...] + jnp.sum(gene_in[...], axis=0)
    tot_out[...] = gene_sum[8:16]

    def to_donors(j, carry):
        pltpu.make_async_remote_copy(
            tot_out, tot_in.at[j - 1], s_sem.at[5], r_sem.at[5],
            device_id={"donor": lax.rem(d + j, 16)}, device_id_type=MESH,
        ).start()
        return carry

    lax.fori_loop(1, 16, to_donors, 0)
    final_out[...] = gene_sum[0:8]
    swap = pltpu.make_async_remote_copy(
        final_out, final_in, s_sem.at[6], r_sem.at[6], device_id=other, device_id_type=MESH
    )
    swap.start()
    swap.wait_recv()
    ours, theirs = final_out[...], final_in[...]
    native_reads = jnp.where(core == 0, ours, theirs)
    contam_reads = jnp.where(core == 0, theirs, ours)
    theta_ref[...] = (contam_reads + BETA) / (native_reads + contam_reads + 2.0 * BETA)
    reads_ref[...] = contam_reads / TOTAL

    wait_for(amb_all.at[fifteen], r_sem.at[4])
    wait_for(tot_in, r_sem.at[5])
    total = jnp.sum(tot_out[...] + jnp.sum(tot_in[...], axis=0), axis=0, keepdims=True)

    def column(wanted, count):
        lanes = lax.broadcasted_iota(jnp.int32, (count, 128), 1)
        rows = lax.broadcasted_iota(jnp.int32, (count, 128), 0)
        return jnp.sum(jnp.where(lanes == wanted(rows), total, 0.0), axis=1, keepdims=True) + TOTAL * PSEUDO

    profile = TOTAL * (both[0:40] + PSEUDO) / column(lambda r: 4 * d + r % 4, 40)
    below = column(lambda r: POPS + r, DONORS)
    ambient = amb_all[...].reshape(128, 128)
    for t in range(10):
        width = min(128, G - 128 * t)
        prof_ref[:, 128 * t : 128 * t + width] = profile[4 * t : 4 * t + 4, 0:width]
        people_rows = TOTAL * (ambient[12 * t : 12 * t + 12] + PSEUDO) / below
        amb_ref[:, 128 * t : 128 * t + width] = people_rows[:, 0:width]

    wait_for(send.at[fifteen, early], s_sem.at[0])
    wait_for(send.at[fifteen, late], s_sem.at[1])
    to_core.wait_send()
    wait_for(gene_in, s_sem.at[3])
    wait_for(amb_all.at[fifteen], s_sem.at[4])
    wait_for(tot_in, s_sem.at[5])
    swap.wait_send()


def body(tallies, blanks, labels, people, members, theta, profiles, ambient):
    hbm = pl.BlockSpec(memory_space=pltpu.HBM)
    vmem = pl.BlockSpec(memory_space=pltpu.VMEM)
    v = pltpu.VMEM
    profile, new_ambient, new_theta, reads = pl.pallas_call(
        kernel,
        out_shape=(
            jax.ShapeDtypeStruct((4, G), f32),
            jax.ShapeDtypeStruct((DONORS, G), f32),
            jax.ShapeDtypeStruct((8, 128), f32),
            jax.ShapeDtypeStruct((8, 128), f32),
        ),
        in_specs=[hbm] * 8,
        out_specs=(vmem,) * 4,
        scratch_shapes=[
            v((G, N), bf16), v((G, NB), bf16), v((1, N), jnp.int32), v((1, N), jnp.int32),
            v((DONORS, 384), jnp.int32), v((1, N), f32), v((POPS, G), f32), v((DONORS, G), f32),
            v((256, N), bf16), v((256, GP), bf16),
            v((16, ROWS, 128), f32), v((15, ROWS, 128), f32), v((24, 128), f32), v((16, 128), f32),
            v((16, 128), f32), v((15, 16, 128), f32), v((8, 128), f32), v((8, 128), f32),
            v((16, 8, 128), f32), v((8, 128), f32), v((15, 8, 128), f32),
            pltpu.SemaphoreType.DMA((12,)), pltpu.SemaphoreType.DMA((7,)), pltpu.SemaphoreType.DMA((7,)),
        ],
        compiler_params=pltpu.CompilerParams(
            collective_id=0, has_side_effects=True, vmem_limit_bytes=56 << 20
        ),
    )(
        tallies.T, blanks.T, labels.reshape(1, N), people.reshape(1, N), members, theta.reshape(1, N),
        profiles, ambient,
    )
    return profile, new_ambient, new_theta.reshape(N), reads.reshape(N)


def solution(mesh):
    in_specs = (
        P("donor", "gene"), P("donor", "gene"), P("donor"), P("donor"), P(), P("donor"),
        P(None, "gene"), P(None, "gene"),
    )
    out_specs = (P("donor", "gene"), P(None, "gene"), P("donor"), P("donor"))
    return jax.shard_map(body, mesh=mesh, in_specs=in_specs, out_specs=out_specs, check_vma=False)
```

```python
import jax
import jax.numpy as jnp
from jax import lax
from jax.experimental import pallas as pl
from jax.experimental.pallas import tpu as pltpu
from jax.sharding import PartitionSpec as P

TOTAL = 40352
PSEUDO = 0.5
BETA = 10.0
G, N, NB, GP = 1261, 1024, 256, 1280
POPS, DONORS = 64, 12
CHUNK = 256
EARLY = 24
ROWS = 48
f32, bf16 = jnp.float32, jnp.bfloat16
MESH = pl.DeviceIdType.MESH
LAST = (((1,), (1,)), ((), ()))
FIRST = (((0,), (0,)), ((), ()))


def thirds(v):
    hi = v.astype(bf16)
    rest = v - hi.astype(f32)
    mid = rest.astype(bf16)
    return hi, mid, (rest - mid.astype(f32)).astype(bf16)


def hot(mask):
    return jnp.where(mask, 1.0, 0.0).astype(bf16)


def padded_tail(ref):
    width = ref.shape[1]
    ragged = jnp.concatenate([ref[1248:G].astype(f32), jnp.zeros((3, width), f32)], axis=0)
    return jnp.concatenate([ref[1024:1248], ragged.astype(bf16), jnp.zeros((16, width), bf16)], axis=0)


def kernel(
    x_hbm, b_hbm, lab_hbm, don_hbm, mem_hbm, th_hbm, e_hbm, p_hbm,
    out_ref,
    xs, bs, lab_v, don_v, mem_v, th_v, e_v, p_v, hots, table,
    send, got, mine, from_core, plane_out, plane_in, pair_out, pair_in, z_out, z_in, final_out, final_in,
    amb_all, tot_out, tot_in,
    in_sem, s_sem, r_sem,
):
    d = lax.axis_index("donor")
    q = lax.axis_index("gene")
    core = lax.rem(q, 2)
    other = {"gene": q + 1 - 2 * core}

    smalls = (
        (lab_hbm, lab_v), (don_hbm, don_v), (th_hbm, th_v), (e_hbm, e_v), (p_hbm, p_v), (mem_hbm, mem_v),
    )
    small_in = [pltpu.make_async_copy(a, b, in_sem.at[i]) for i, (a, b) in enumerate(smalls)]
    for c in small_in:
        c.start()
    x_in = []
    for c in range(5):
        rows = pl.ds(CHUNK * c, min(CHUNK, G - CHUNK * c))
        x_in.append(pltpu.make_async_copy(x_hbm.at[rows], xs.at[rows], in_sem.at[6 + c]))
    b_in = pltpu.make_async_copy(b_hbm, bs, in_sem.at[11])
    for c in x_in[:1] + [b_in] + x_in[1:]:
        c.start()

    barrier = pltpu.get_barrier_semaphore()
    y_hi = lax.rem(q // 2, 2)
    place = 2 * d + y_hi

    def plane_peer(j):
        to = lax.rem(place + j, 32)
        return {"donor": to // 2, "gene": q + 2 * (lax.rem(to, 2) - y_hi)}

    def z_peer(j):
        return {"gene": lax.rem(q + 4 * j, 32)}

    def greet_z(j, carry):
        pl.semaphore_signal(barrier, inc=1, device_id=z_peer(j), device_id_type=MESH)
        return carry

    def greet_plane(j, carry):
        pl.semaphore_signal(barrier, inc=1, device_id=plane_peer(j), device_id_type=MESH)
        return carry

    lax.fori_loop(1, 8, greet_z, 0)
    lax.fori_loop(1, 32, greet_plane, 0)
    pl.semaphore_signal(barrier, inc=1, device_id=other, device_id_type=MESH)

    for c in small_in:
        c.wait()
    labels, people, theta = lab_v[...], don_v[...], th_v[...]
    pop_hot = hot(labels == lax.broadcasted_iota(jnp.int32, (POPS, N), 0))
    donor_hot = hot(people == lax.broadcasted_iota(jnp.int32, (16, N), 0))
    for i in range(3):
        hots[64 * i : 64 * i + 64] = pop_hot
        hots[192 + 16 * i : 208 + 16 * i] = donor_hot
    row = lax.broadcasted_iota(jnp.int32, (16, N), 0)
    odds = jnp.zeros((16, N), f32)
    for i, v in enumerate(thirds((jnp.log(theta) - jnp.log(1.0 - theta)) * -0.5)):
        odds = jnp.where(row == i, v.astype(f32), odds)
    hots[240:256] = odds.astype(bf16)
    for i, v in enumerate(thirds(jnp.log(e_v[...]) * 0.5)):
        table[64 * i : 64 * i + 64, 0:G] = v
    log_ambient = jnp.concatenate([jnp.log(p_v[...]) * -0.5, jnp.zeros((4, G), f32)], axis=0)
    for i, v in enumerate(thirds(log_ambient)):
        table[192 + 16 * i : 208 + 16 * i, 0:G] = v
    table[240:256] = hot(lax.broadcasted_iota(jnp.int32, (16, GP), 0) < 3)
    table[0:240, G:GP] = jnp.zeros((240, GP - G), bf16)

    members = mem_v[...] - d * NB
    empties = lax.broadcasted_iota(jnp.int32, (NB, 128), 0)
    lane = lax.broadcasted_iota(jnp.int32, (128, 128), 1)
    listed = jnp.zeros((NB, 128), f32)
    for r in range(DONORS):
        count = jnp.zeros((NB, 128), f32)
        for t in range(3):
            count = count + jnp.where(members[r : r + 1, 128 * t : 128 * t + 128] == empties, 1.0, 0.0)
        listed = listed + jnp.dot(count.astype(bf16), hot(lane == POPS + r), preferred_element_type=f32)
    listed_hi = listed.astype(bf16)
    listed_lo = (listed - listed_hi.astype(f32)).astype(bf16)

    pops = jnp.concatenate([pop_hot, jnp.zeros((64, N), bf16)], axis=0)
    folk = jnp.concatenate([jnp.zeros((64, N), bf16), donor_hot, jnp.zeros((48, N), bf16)], axis=0)
    send[15, 40:48] = jnp.zeros((8, 128), f32)

    native_acc = jnp.zeros((8, N), f32)
    contam_acc = jnp.zeros((8, N), f32)
    totals = jnp.zeros((8, 128), f32)

    def spread(first, count, index):
        def one(j, carry):
            peer = lax.rem(d + j, 16)
            pltpu.make_async_remote_copy(
                send.at[peer, pl.ds(first, count)], got.at[j - 1, pl.ds(first, count)],
                s_sem.at[index], r_sem.at[index], device_id={"donor": peer}, device_id_type=MESH,
            ).start()
            return carry

        lax.fori_loop(1, 16, one, 0)

    for c in range(5):
        log_odds = lax.dot_general(table[:, CHUNK * c : CHUNK * c + CHUNK], hots[...], FIRST, preferred_element_type=f32)
        x_in[c].wait()
        if c == 0:
            b_in.wait()
        if c < 4:
            counts, blanks = xs[CHUNK * c : CHUNK * c + CHUNK], bs[CHUNK * c : CHUNK * c + CHUNK]
        else:
            counts, blanks = padded_tail(xs), padded_tail(bs)
        half = counts.astype(f32) * 0.5
        swing = half * jnp.tanh(log_odds)
        native = (half + swing).astype(bf16)
        contam = (half - swing).astype(bf16)
        native_acc = native_acc + jnp.sum(native.astype(f32).reshape(CHUNK // 8, 8, N), axis=0)
        contam_acc = contam_acc + jnp.sum(contam.astype(f32).reshape(CHUNK // 8, 8, N), axis=0)
        sums = lax.dot_general(native, pops, LAST, preferred_element_type=f32)
        sums = sums + lax.dot_general(contam, folk, LAST, preferred_element_type=f32)
        sums = sums + jnp.dot(blanks, listed_hi, preferred_element_type=f32)
        sums = sums + jnp.dot(blanks, listed_lo, preferred_element_type=f32)
        totals = totals + jnp.sum(sums.reshape(CHUNK // 8, 8, 128), axis=0)
        for h in range(2):
            t = 2 * c + h
            turned = sums[128 * h : 128 * h + 128].T
            for i in range(16):
                send[i, 4 * t : 4 * t + 4] = turned[4 * i : 4 * i + 4]
            r = 0
            while r < DONORS:
                u = 12 * t + r
                run = min(DONORS - r, 8 - u % 8)
                send[u // 8, 40 + u % 8 : 40 + u % 8 + run] = turned[64 + r : 64 + r + run]
                r += run
        if c == 2:
            pl.semaphore_wait(barrier, 39)
            spread(0, EARLY, 0)

    native_row = jnp.sum(native_acc, axis=0, keepdims=True)
    contam_row = jnp.sum(contam_acc, axis=0, keepdims=True)
    for i in range(8):
        mine[i : i + 1] = native_row[:, 128 * i : 128 * i + 128]
        mine[16 + i : 17 + i] = contam_row[:, 128 * i : 128 * i + 128]
    mine[8:16] = totals
    to_core = pltpu.make_async_remote_copy(
        mine.at[pl.ds(8 - 8 * core, 16)], from_core, s_sem.at[2], r_sem.at[2], device_id=other, device_id_type=MESH
    )
    to_core.start()
    spread(40, 8, 1)

    to_core.wait_recv()
    at_reads = pl.multiple_of(8 * core, 8)
    at_total = pl.multiple_of(8 - 8 * core, 8)
    plane_out[...] = jnp.sum(mine[8:16] + from_core[pl.ds(at_total, 8)], axis=0, keepdims=True)
    pair_out[...] = mine[pl.ds(pl.multiple_of(16 * core, 8), 8)] + from_core[pl.ds(at_reads, 8)]

    def to_plane(j, carry):
        pltpu.make_async_remote_copy(
            plane_out, plane_in.at[j - 1], s_sem.at[3], r_sem.at[3], device_id=plane_peer(j), device_id_type=MESH
        ).start()
        return carry

    across = pltpu.make_async_remote_copy(
        pair_out, pair_in, s_sem.at[4], r_sem.at[4], device_id={"gene": q + 2 - 4 * y_hi}, device_id_type=MESH
    )
    across.start()
    lax.fori_loop(1, 32, to_plane, 0)
    spread(EARLY, 40 - EARLY, 5)

    across.wait_recv()
    z_out[...] = pair_out[...] + pair_in[...]

    def to_z(j, carry):
        pltpu.make_async_remote_copy(
            z_out, z_in.at[j - 1], s_sem.at[6], r_sem.at[6], device_id=z_peer(j), device_id_type=MESH
        ).start()
        return carry

    lax.fori_loop(1, 8, to_z, 0)

    def wait_for(ref, sem):
        pltpu.make_async_copy(ref, ref, sem).wait()

    fifteen = pl.ds(0, 15)
    wait_for(got.at[fifteen, pl.ds(40, 8)], r_sem.at[1])
    amb_all[d] = send[d, 40:48] + jnp.sum(got[:, 40:48], axis=0)

    def to_all(j, carry):
        pltpu.make_async_remote_copy(
            amb_all.at[d], amb_all.at[d], s_sem.at[7], r_sem.at[7],
            device_id={"donor": lax.rem(d + j, 16)}, device_id_type=MESH,
        ).start()
        return carry

    lax.fori_loop(1, 16, to_all, 0)

    wait_for(plane_in, r_sem.at[3])
    tot_out[...] = plane_out[...] + jnp.sum(plane_in[...], axis=0)

    def total_to_z(j, carry):
        pltpu.make_async_remote_copy(
            tot_out, tot_in.at[j - 1], s_sem.at[8], r_sem.at[8], device_id=z_peer(j), device_id_type=MESH
        ).start()
        return carry

    lax.fori_loop(1, 8, total_to_z, 0)

    wait_for(z_in, r_sem.at[6])
    final_out[...] = z_out[...] + jnp.sum(z_in[...], axis=0)
    swap = pltpu.make_async_remote_copy(
        final_out, final_in, s_sem.at[9], r_sem.at[9], device_id=other, device_id_type=MESH
    )
    swap.start()

    wait_for(got.at[fifteen, pl.ds(0, EARLY)], r_sem.at[0])
    wait_for(got.at[fifteen, pl.ds(EARLY, 40 - EARLY)], r_sem.at[5])
    pop_sums = send[d, 0:40] + jnp.sum(got[:, 0:40], axis=0)

    swap.wait_recv()
    ours, theirs = final_out[...], final_in[...]
    native_reads = jnp.where(core == 0, ours, theirs)
    contam_reads = jnp.where(core == 0, theirs, ours)
    out_ref[0:8] = (contam_reads + BETA) / (native_reads + contam_reads + 2.0 * BETA)
    out_ref[8:16] = contam_reads / TOTAL

    wait_for(amb_all.at[fifteen], r_sem.at[7])
    ambient = amb_all[...].reshape(128, 128)
    wait_for(tot_in, r_sem.at[8])
    total = tot_out[...] + jnp.sum(tot_in[...], axis=0)

    def column(wanted, count):
        lanes = lax.broadcasted_iota(jnp.int32, (count, 128), 1)
        rows = lax.broadcasted_iota(jnp.int32, (count, 128), 0)
        return jnp.sum(jnp.where(lanes == wanted(rows), total, 0.0), axis=1, keepdims=True) + TOTAL * PSEUDO

    out_ref[16:56] = TOTAL * (pop_sums + PSEUDO) / column(lambda r: 4 * d + r % 4, 40)
    out_ref[56:184] = TOTAL * (ambient + PSEUDO) / column(lambda r: POPS + r % DONORS, 128)

    wait_for(send.at[fifteen, pl.ds(0, EARLY)], s_sem.at[0])
    wait_for(send.at[fifteen, pl.ds(40, 8)], s_sem.at[1])
    wait_for(send.at[fifteen, pl.ds(EARLY, 40 - EARLY)], s_sem.at[5])
    to_core.wait_send()
    wait_for(plane_in, s_sem.at[3])
    across.wait_send()
    wait_for(z_in, s_sem.at[6])
    wait_for(amb_all.at[fifteen], s_sem.at[7])
    wait_for(tot_in, s_sem.at[8])
    swap.wait_send()


def finish(raw_ref, prof_ref, amb_ref, theta_ref, reads_ref):
    theta_ref[...] = raw_ref[0:8]
    reads_ref[...] = raw_ref[8:16]
    for t in range(10):
        width = min(128, G - 128 * t)
        prof_ref[:, 128 * t : 128 * t + width] = raw_ref[16 + 4 * t : 20 + 4 * t, 0:width]
        amb_ref[:, 128 * t : 128 * t + width] = raw_ref[56 + 12 * t : 68 + 12 * t, 0:width]


def body(tallies, blanks, labels, people, members, theta, profiles, ambient):
    hbm = pl.BlockSpec(memory_space=pltpu.HBM)
    vmem = pl.BlockSpec(memory_space=pltpu.VMEM)
    v = pltpu.VMEM
    raw = pl.pallas_call(
        kernel,
        out_shape=jax.ShapeDtypeStruct((184, 128), f32),
        in_specs=[hbm] * 8,
        out_specs=vmem,
        scratch_shapes=[
            v((G, N), bf16), v((G, NB), bf16), v((1, N), jnp.int32), v((1, N), jnp.int32),
            v((DONORS, 384), jnp.int32), v((1, N), f32), v((POPS, G), f32), v((DONORS, G), f32),
            v((256, N), bf16), v((256, GP), bf16),
            v((16, ROWS, 128), f32), v((15, ROWS, 128), f32), v((24, 128), f32), v((16, 128), f32),
            v((1, 128), f32), v((31, 1, 128), f32), v((8, 128), f32), v((8, 128), f32),
            v((8, 128), f32), v((7, 8, 128), f32), v((8, 128), f32), v((8, 128), f32),
            v((16, 8, 128), f32), v((1, 128), f32), v((7, 1, 128), f32),
            pltpu.SemaphoreType.DMA((12,)), pltpu.SemaphoreType.DMA((10,)), pltpu.SemaphoreType.DMA((10,)),
        ],
        compiler_params=pltpu.CompilerParams(
            collective_id=0, has_side_effects=True, vmem_limit_bytes=56 << 20
        ),
    )(
        tallies.T, blanks.T, labels.reshape(1, N), people.reshape(1, N), members, theta.reshape(1, N),
        profiles, ambient,
    )
    profile, new_ambient, new_theta, reads = pl.pallas_call(
        finish,
        out_shape=(
            jax.ShapeDtypeStruct((4, G), f32),
            jax.ShapeDtypeStruct((DONORS, G), f32),
            jax.ShapeDtypeStruct((8, 128), f32),
            jax.ShapeDtypeStruct((8, 128), f32),
        ),
        in_specs=[vmem],
        out_specs=(vmem,) * 4,
    )(raw)
    return profile, new_ambient, new_theta.reshape(N), reads.reshape(N)


def solution(mesh):
    in_specs = (
        P("donor", "gene"), P("donor", "gene"), P("donor"), P("donor"), P(), P("donor"),
        P(None, "gene"), P(None, "gene"),
    )
    out_specs = (P("donor", "gene"), P(None, "gene"), P("donor"), P("donor"))
    return jax.shard_map(body, mesh=mesh, in_specs=in_specs, out_specs=out_specs, check_vma=False)
```

```python
import jax
import jax.numpy as jnp
from jax import lax
from jax.experimental import pallas as pl
from jax.experimental.pallas import tpu as pltpu
from jax.sharding import PartitionSpec as P

TOTAL = 40352
PSEUDO = 0.5
BETA = 10.0
G, N, NB, GP = 1261, 1024, 256, 1280
POPS, DONORS = 64, 12
CHUNK = 256
EARLY = 3
f32, bf16 = jnp.float32, jnp.bfloat16
MESH = pl.DeviceIdType.MESH
LAST = (((1,), (1,)), ((), ()))
FIRST = (((0,), (0,)), ((), ()))


def thirds(v):
    hi = v.astype(bf16)
    rest = v - hi.astype(f32)
    mid = rest.astype(bf16)
    return hi, mid, (rest - mid.astype(f32)).astype(bf16)


def hot(mask):
    return jnp.where(mask, 1.0, 0.0).astype(bf16)


def padded_tail(ref):
    width = ref.shape[1]
    ragged = jnp.concatenate([ref[1248:G].astype(f32), jnp.zeros((3, width), f32)], axis=0)
    return jnp.concatenate([ref[1024:1248], ragged.astype(bf16), jnp.zeros((16, width), bf16)], axis=0)


def kernel(
    x_hbm, b_hbm, lab_hbm, don_hbm, mem_hbm, th_hbm, e_hbm, p_hbm,
    out_ref,
    xs, bs, lab_v, don_v, mem_v, th_v, e_v, p_v, hots, table,
    pop_send, x_got, y_send, y_got, amb_send, amb_got, amb_all, mine, from_core, pair_out, pair_in, z_out, z_in,
    plane_out, plane_in, tot_out, tot_in,
    in_sem, s_sem, r_sem,
):
    d = lax.axis_index("donor")
    q = lax.axis_index("gene")
    core = lax.rem(q, 2)
    other = {"gene": q + 1 - 2 * core}

    smalls = (
        (lab_hbm, lab_v), (don_hbm, don_v), (th_hbm, th_v), (e_hbm, e_v), (p_hbm, p_v), (mem_hbm, mem_v),
    )
    small_in = [pltpu.make_async_copy(a, b, in_sem.at[i]) for i, (a, b) in enumerate(smalls)]
    for c in small_in:
        c.start()
    x_in = []
    for c in range(5):
        rows = pl.ds(CHUNK * c, min(CHUNK, G - CHUNK * c))
        x_in.append(pltpu.make_async_copy(x_hbm.at[rows], xs.at[rows], in_sem.at[6 + c]))
    b_in = pltpu.make_async_copy(b_hbm, bs, in_sem.at[11])
    for c in x_in[:1] + [b_in] + x_in[1:]:
        c.start()

    barrier = pltpu.get_barrier_semaphore()
    y_hi = lax.rem(q // 2, 2)
    place = 2 * d + y_hi

    def plane_peer(j):
        to = lax.rem(place + j, 32)
        return {"donor": to // 2, "gene": q + 2 * (lax.rem(to, 2) - y_hi)}

    spot = 2 * (q // 4) + core

    def z_peer(j):
        to = lax.rem(spot + j, 16)
        return {"gene": 4 * (to // 2) + 2 * y_hi + lax.rem(to, 2)}

    def far_first(i, middle):
        return middle + (i + 1) // 2 * (1 - 2 * lax.rem(i, 2))

    def signal_to(peer):
        pl.semaphore_signal(barrier, inc=1, device_id=peer, device_id_type=MESH)

    def greet_z(i, carry):
        signal_to(z_peer(far_first(i, 8)))
        return carry

    def greet_plane(i, carry):
        signal_to(plane_peer(far_first(i, 16)))
        return carry

    lax.fori_loop(0, 15, greet_z, 0)
    lax.fori_loop(0, 31, greet_plane, 0)

    for c in small_in:
        c.wait()
    labels, people, theta = lab_v[...], don_v[...], th_v[...]
    pop_hot = hot(labels == lax.broadcasted_iota(jnp.int32, (POPS, N), 0))
    donor_hot = hot(people == lax.broadcasted_iota(jnp.int32, (16, N), 0))
    for i in range(3):
        hots[64 * i : 64 * i + 64] = pop_hot
        hots[192 + 16 * i : 208 + 16 * i] = donor_hot
    row = lax.broadcasted_iota(jnp.int32, (16, N), 0)
    odds = jnp.zeros((16, N), f32)
    for i, v in enumerate(thirds((jnp.log(theta) - jnp.log(1.0 - theta)) * -0.5)):
        odds = jnp.where(row == i, v.astype(f32), odds)
    hots[240:256] = odds.astype(bf16)
    for i, v in enumerate(thirds(jnp.log(e_v[...]) * 0.5)):
        table[64 * i : 64 * i + 64, 0:G] = v
    log_ambient = jnp.concatenate([jnp.log(p_v[...]) * -0.5, jnp.zeros((4, G), f32)], axis=0)
    for i, v in enumerate(thirds(log_ambient)):
        table[192 + 16 * i : 208 + 16 * i, 0:G] = v
    table[240:256] = hot(lax.broadcasted_iota(jnp.int32, (16, GP), 0) < 3)
    table[0:240, G:GP] = jnp.zeros((240, GP - G), bf16)

    members = mem_v[...] - d * NB
    empties = lax.broadcasted_iota(jnp.int32, (NB, 128), 0)
    lane = lax.broadcasted_iota(jnp.int32, (128, 128), 1)
    listed = jnp.zeros((NB, 128), f32)
    for r in range(DONORS):
        count = jnp.zeros((NB, 128), f32)
        for t in range(3):
            count = count + jnp.where(members[r : r + 1, 128 * t : 128 * t + 128] == empties, 1.0, 0.0)
        listed = listed + jnp.dot(count.astype(bf16), hot(lane == POPS + r), preferred_element_type=f32)
    listed_hi = listed.astype(bf16)
    listed_lo = (listed - listed_hi.astype(f32)).astype(bf16)

    listed_both = jnp.concatenate([listed_hi, listed_lo], axis=1)
    pops = jnp.concatenate([pop_hot, jnp.zeros((64, N), bf16)], axis=0)
    folk = jnp.concatenate([jnp.zeros((64, N), bf16), donor_hot, jnp.zeros((48, N), bf16)], axis=0)
    amb_send[15] = jnp.zeros((8, 128), f32)

    native_acc = jnp.zeros((8, N), f32)
    contam_acc = jnp.zeros((8, N), f32)
    totals = jnp.zeros((8, 128), f32)

    x_at, y_at = d // 4, lax.rem(d, 4)

    def to_x(first, count, index):
        copies = []
        for j in (2, 1, 3):
            there = lax.rem(x_at + j, 4)
            copies.append(
                pltpu.make_async_remote_copy(
                    pop_send.at[there, pl.ds(first, count)], x_got.at[j - 1, pl.ds(first, count)],
                    s_sem.at[index], r_sem.at[index], device_id={"donor": 4 * there + y_at}, device_id_type=MESH,
                )
            )
            copies[-1].start()
        return copies

    def look_up(c):
        part = table[:, CHUNK * c : CHUNK * c + CHUNK]
        return lax.dot_general(part, hots[...], FIRST, preferred_element_type=f32)

    for c in x_in[:EARLY] + [b_in]:
        c.wait()
    ahead = look_up(0)
    for c in range(5):
        log_odds = ahead
        if c < 4:
            ahead = look_up(c + 1)
        if c < 4:
            counts, blanks = xs[CHUNK * c : CHUNK * c + CHUNK], bs[CHUNK * c : CHUNK * c + CHUNK]
        else:
            counts, blanks = padded_tail(xs), padded_tail(bs)
        half = counts.astype(f32) * 0.5
        swing = half * jnp.tanh(log_odds)
        native = (half + swing).astype(bf16)
        contam = (half - swing).astype(bf16)
        native_acc = native_acc + jnp.sum(native.astype(f32).reshape(CHUNK // 8, 8, N), axis=0)
        contam_acc = contam_acc + jnp.sum(contam.astype(f32).reshape(CHUNK // 8, 8, N), axis=0)
        sums = lax.dot_general(native, pops, LAST, preferred_element_type=f32)
        sums = sums + lax.dot_general(contam, folk, LAST, preferred_element_type=f32)
        extra = jnp.dot(blanks, listed_both, preferred_element_type=f32)
        sums = sums + (extra[:, 0:128] + extra[:, 128:256])
        totals = totals + jnp.sum(sums.reshape(CHUNK // 8, 8, 128), axis=0)
        for h in range(2):
            t = 2 * c + h
            turned = sums[128 * h : 128 * h + 128].T
            for i in range(16):
                pop_send[i // 4, c, i % 4, 4 * h : 4 * h + 4] = turned[4 * i : 4 * i + 4]
            r = 0
            while r < DONORS:
                u = 12 * t + r
                run = min(DONORS - r, 8 - u % 8)
                amb_send[u // 8, u % 8 : u % 8 + run] = turned[64 + r : 64 + r + run]
                r += run
        if c == EARLY - 1:
            pl.semaphore_wait(barrier, 46)
            to_x(0, EARLY, 0)
            for e in x_in[EARLY:]:
                e.wait()

    plane_out[...] = jnp.sum(totals, axis=0, keepdims=True)
    native_row = jnp.sum(native_acc, axis=0, keepdims=True)
    contam_row = jnp.sum(contam_acc, axis=0, keepdims=True)
    for i in range(8):
        mine[0, i : i + 1] = native_row[:, 128 * i : 128 * i + 128]
        mine[1, i : i + 1] = contam_row[:, 128 * i : 128 * i + 128]
    to_core = pltpu.make_async_remote_copy(
        mine.at[1 - core], from_core, s_sem.at[2], r_sem.at[2], device_id=other, device_id_type=MESH
    )
    to_core.start()

    def to_plane(i, carry):
        j = far_first(i, 16)
        pltpu.make_async_remote_copy(
            plane_out, plane_in.at[j - 1], s_sem.at[3], r_sem.at[3], device_id=plane_peer(j), device_id_type=MESH
        ).start()
        return carry

    lax.fori_loop(0, 31, to_plane, 0)
    to_core.wait_recv()
    pair_out[...] = mine[core] + from_core[...]
    across = pltpu.make_async_remote_copy(
        pair_out, pair_in, s_sem.at[4], r_sem.at[4], device_id={"gene": q + 2 - 4 * y_hi}, device_id_type=MESH
    )
    across.start()

    def to_owner(j, carry):
        peer = lax.rem(d + j, 16)
        pltpu.make_async_remote_copy(
            amb_send.at[peer], amb_got.at[j - 1], s_sem.at[1], r_sem.at[1],
            device_id={"donor": peer}, device_id_type=MESH,
        ).start()
        return carry

    lax.fori_loop(1, 16, to_owner, 0)
    to_x(EARLY, 5 - EARLY, 5)

    across.wait_recv()
    z_out[...] = pair_out[...] + pair_in[...]

    def to_z(i, carry):
        j = far_first(i, 8)
        pltpu.make_async_remote_copy(
            z_out, z_in.at[j - 1], s_sem.at[6], r_sem.at[6], device_id=z_peer(j), device_id_type=MESH
        ).start()
        return carry

    lax.fori_loop(0, 15, to_z, 0)

    def wait_for(ref, sem):
        pltpu.make_async_copy(ref, ref, sem).wait()

    wait_for(plane_in, r_sem.at[3])
    tot_out[...] = plane_out[...] + jnp.sum(plane_in[...], axis=0)

    def total_to_z(i, carry):
        j = far_first(i, 8)
        pltpu.make_async_remote_copy(
            tot_out, tot_in.at[j - 1], s_sem.at[8], r_sem.at[8], device_id=z_peer(j), device_id_type=MESH
        ).start()
        return carry

    lax.fori_loop(0, 15, total_to_z, 0)

    wait_for(amb_got, r_sem.at[1])
    amb_all[d] = amb_send[d] + jnp.sum(amb_got[...], axis=0)

    def to_all(j, carry):
        pltpu.make_async_remote_copy(
            amb_all.at[d], amb_all.at[d], s_sem.at[7], r_sem.at[7],
            device_id={"donor": lax.rem(d + j, 16)}, device_id_type=MESH,
        ).start()
        return carry

    lax.fori_loop(1, 16, to_all, 0)

    three = pl.ds(0, 3)
    wait_for(x_got.at[three, pl.ds(0, EARLY)], r_sem.at[0])
    wait_for(x_got.at[three, pl.ds(EARLY, 5 - EARLY)], r_sem.at[5])
    y_send[...] = pop_send[x_at] + jnp.sum(x_got[...], axis=0)
    to_y = []
    for j in (2, 1, 3):
        there = lax.rem(y_at + j, 4)
        to_y.append(
            pltpu.make_async_remote_copy(
                y_send.at[:, there], y_got.at[j - 1], s_sem.at[9], r_sem.at[9],
                device_id={"donor": 4 * x_at + there}, device_id_type=MESH,
            )
        )
        to_y[-1].start()

    wait_for(z_in, r_sem.at[6])
    ours, theirs = z_out[...], z_in[0]
    for j in range(2, 16):
        if j % 2:
            theirs = theirs + z_in[j - 1]
        else:
            ours = ours + z_in[j - 1]
    native_reads = jnp.where(core == 0, ours, theirs)
    contam_reads = jnp.where(core == 0, theirs, ours)
    out_ref[0:8] = (contam_reads + BETA) / (native_reads + contam_reads + 2.0 * BETA)
    out_ref[8:16] = contam_reads / TOTAL

    wait_for(y_got, r_sem.at[9])
    pop_sums = (y_send[:, y_at] + jnp.sum(y_got[...], axis=0)).reshape(40, 128)
    wait_for(amb_all.at[pl.ds(0, 15)], r_sem.at[7])
    ambient = amb_all[...].reshape(128, 128)
    wait_for(tot_in, r_sem.at[8])
    total = tot_out[...] + jnp.sum(tot_in[...], axis=0)

    def column(wanted, count):
        lanes = lax.broadcasted_iota(jnp.int32, (count, 128), 1)
        rows = lax.broadcasted_iota(jnp.int32, (count, 128), 0)
        return jnp.sum(jnp.where(lanes == wanted(rows), total, 0.0), axis=1, keepdims=True) + TOTAL * PSEUDO

    out_ref[16:56] = TOTAL * (pop_sums + PSEUDO) / column(lambda r: 4 * d + r % 4, 40)
    out_ref[56:184] = TOTAL * (ambient + PSEUDO) / column(lambda r: POPS + r % DONORS, 128)

    wait_for(x_got.at[three, pl.ds(0, EARLY)], s_sem.at[0])
    wait_for(x_got.at[three, pl.ds(EARLY, 5 - EARLY)], s_sem.at[5])
    wait_for(amb_got, s_sem.at[1])
    to_core.wait_send()
    wait_for(plane_in, s_sem.at[3])
    across.wait_send()
    wait_for(z_in, s_sem.at[6])
    wait_for(amb_all.at[pl.ds(0, 15)], s_sem.at[7])
    wait_for(tot_in, s_sem.at[8])
    wait_for(y_got, s_sem.at[9])


def finish(raw_ref, prof_ref, amb_ref, theta_ref, reads_ref):
    theta_ref[...] = raw_ref[0:8]
    reads_ref[...] = raw_ref[8:16]
    for t in range(10):
        width = min(128, G - 128 * t)
        prof_ref[:, 128 * t : 128 * t + width] = raw_ref[16 + 4 * t : 20 + 4 * t, 0:width]
        amb_ref[:, 128 * t : 128 * t + width] = raw_ref[56 + 12 * t : 68 + 12 * t, 0:width]


def body(tallies, blanks, labels, people, members, theta, profiles, ambient):
    hbm = pl.BlockSpec(memory_space=pltpu.HBM)
    vmem = pl.BlockSpec(memory_space=pltpu.VMEM)
    v = pltpu.VMEM
    raw = pl.pallas_call(
        kernel,
        out_shape=jax.ShapeDtypeStruct((184, 128), f32),
        in_specs=[hbm] * 8,
        out_specs=vmem,
        scratch_shapes=[
            v((G, N), bf16), v((G, NB), bf16), v((1, N), jnp.int32), v((1, N), jnp.int32),
            v((DONORS, 384), jnp.int32), v((1, N), f32), v((POPS, G), f32), v((DONORS, G), f32),
            v((256, N), bf16), v((256, GP), bf16),
            v((4, 5, 4, 8, 128), f32), v((3, 5, 4, 8, 128), f32), v((5, 4, 8, 128), f32), v((3, 5, 8, 128), f32),
            v((16, 8, 128), f32), v((15, 8, 128), f32), v((16, 8, 128), f32),
            v((2, 8, 128), f32), v((8, 128), f32), v((8, 128), f32), v((8, 128), f32), v((8, 128), f32),
            v((15, 8, 128), f32), v((1, 128), f32), v((31, 1, 128), f32), v((1, 128), f32), v((15, 1, 128), f32),
            pltpu.SemaphoreType.DMA((12,)), pltpu.SemaphoreType.DMA((10,)), pltpu.SemaphoreType.DMA((10,)),
        ],
        compiler_params=pltpu.CompilerParams(
            collective_id=0, has_side_effects=True, vmem_limit_bytes=56 << 20
        ),
    )(
        tallies.T, blanks.T, labels.reshape(1, N), people.reshape(1, N), members, theta.reshape(1, N),
        profiles, ambient,
    )
    profile, new_ambient, new_theta, reads = pl.pallas_call(
        finish,
        out_shape=(
            jax.ShapeDtypeStruct((4, G), f32),
            jax.ShapeDtypeStruct((DONORS, G), f32),
            jax.ShapeDtypeStruct((8, 128), f32),
            jax.ShapeDtypeStruct((8, 128), f32),
        ),
        in_specs=[vmem],
        out_specs=(vmem,) * 4,
    )(raw)
    return profile, new_ambient, new_theta.reshape(N), reads.reshape(N)


def solution(mesh):
    in_specs = (
        P("donor", "gene"), P("donor", "gene"), P("donor"), P("donor"), P(), P("donor"),
        P(None, "gene"), P(None, "gene"),
    )
    out_specs = (P("donor", "gene"), P(None, "gene"), P("donor"), P("donor"))
    return jax.shard_map(body, mesh=mesh, in_specs=in_specs, out_specs=out_specs, check_vma=False)
```

```python
import jax
import jax.numpy as jnp
from jax import lax
from jax.experimental import pallas as pl
from jax.experimental.pallas import tpu as pltpu
from jax.sharding import PartitionSpec as P

TOTAL = 40352
PSEUDO = 0.5
BETA = 10.0
G, N, NB, GP = 1261, 1024, 256, 1280
POPS, DONORS = 64, 12
CHUNK = 256
EARLY = 3
f32, bf16 = jnp.float32, jnp.bfloat16
MESH = pl.DeviceIdType.MESH
LAST = (((1,), (1,)), ((), ()))
FIRST = (((0,), (0,)), ((), ()))


def thirds(v):
    hi = v.astype(bf16)
    rest = v - hi.astype(f32)
    mid = rest.astype(bf16)
    return hi, mid, (rest - mid.astype(f32)).astype(bf16)


def hot(mask):
    return jnp.where(mask, 1.0, 0.0).astype(bf16)


def padded_tail(ref):
    width = ref.shape[1]
    ragged = jnp.concatenate([ref[1248:G].astype(f32), jnp.zeros((3, width), f32)], axis=0)
    return jnp.concatenate([ref[1024:1248], ragged.astype(bf16), jnp.zeros((16, width), bf16)], axis=0)


def kernel(
    x_hbm, b_hbm, lab_hbm, don_hbm, mem_hbm, th_hbm, e_hbm, p_hbm,
    out_ref,
    xs, bs, lab_v, don_v, mem_v, th_v, e_v, p_v, hots, table,
    pop_send, x_got, y_send, y_got, amb_send, amb_got, amb_all, mine, from_core, pair_out, pair_in, z_out, z_in,
    plane_out, plane_in, tot_out, tot_in,
    in_sem, s_sem, r_sem,
):
    d = lax.axis_index("donor")
    q = lax.axis_index("gene")
    core = lax.rem(q, 2)
    other = {"gene": q + 1 - 2 * core}

    smalls = (
        (lab_hbm, lab_v), (don_hbm, don_v), (th_hbm, th_v), (e_hbm, e_v), (p_hbm, p_v), (mem_hbm, mem_v),
    )
    small_in = [pltpu.make_async_copy(a, b, in_sem.at[i]) for i, (a, b) in enumerate(smalls)]
    for c in small_in:
        c.start()
    x_in = []
    for c in range(5):
        rows = pl.ds(CHUNK * c, min(CHUNK, G - CHUNK * c))
        x_in.append(pltpu.make_async_copy(x_hbm.at[rows], xs.at[rows], in_sem.at[6 + c]))
    b_in = pltpu.make_async_copy(b_hbm, bs, in_sem.at[11])
    for c in x_in[:1] + [b_in] + x_in[1:]:
        c.start()

    barrier = pltpu.get_barrier_semaphore()
    y_hi = lax.rem(q // 2, 2)
    place = 2 * d + y_hi

    def plane_peer(j):
        to = lax.rem(place + j, 32)
        return {"donor": to // 2, "gene": q + 2 * (lax.rem(to, 2) - y_hi)}

    spot = 2 * (q // 4) + core

    def z_peer(j):
        to = lax.rem(spot + j, 16)
        return {"gene": 4 * (to // 2) + 2 * y_hi + lax.rem(to, 2)}

    def far_first(i, middle):
        return middle + (i + 1) // 2 * (1 - 2 * lax.rem(i, 2))

    def signal_to(peer):
        pl.semaphore_signal(barrier, inc=1, device_id=peer, device_id_type=MESH)

    def greet_z(i, carry):
        signal_to(z_peer(far_first(i, 8)))
        return carry

    def greet_plane(i, carry):
        signal_to(plane_peer(far_first(i, 16)))
        return carry

    lax.fori_loop(0, 31, greet_plane, 0)
    lax.fori_loop(0, 15, greet_z, 0)

    for c in small_in:
        c.wait()
    labels, people, theta = lab_v[...], don_v[...], th_v[...]
    pop_hot = hot(labels == lax.broadcasted_iota(jnp.int32, (POPS, N), 0))
    donor_hot = hot(people == lax.broadcasted_iota(jnp.int32, (16, N), 0))
    for i in range(3):
        hots[64 * i : 64 * i + 64] = pop_hot
        hots[192 + 16 * i : 208 + 16 * i] = donor_hot
    row = lax.broadcasted_iota(jnp.int32, (16, N), 0)
    odds = jnp.zeros((16, N), f32)
    for i, v in enumerate(thirds((jnp.log(theta) - jnp.log(1.0 - theta)) * -0.5)):
        odds = jnp.where(row == i, v.astype(f32), odds)
    hots[240:256] = odds.astype(bf16)
    for i, v in enumerate(thirds(jnp.log(e_v[...]) * 0.5)):
        table[64 * i : 64 * i + 64, 0:G] = v
    log_ambient = jnp.concatenate([jnp.log(p_v[...]) * -0.5, jnp.zeros((4, G), f32)], axis=0)
    for i, v in enumerate(thirds(log_ambient)):
        table[192 + 16 * i : 208 + 16 * i, 0:G] = v
    table[240:256] = hot(lax.broadcasted_iota(jnp.int32, (16, GP), 0) < 3)
    table[0:240, G:GP] = jnp.zeros((240, GP - G), bf16)

    members = mem_v[...] - d * NB
    empties = lax.broadcasted_iota(jnp.int32, (NB, 128), 0)
    lane = lax.broadcasted_iota(jnp.int32, (128, 128), 1)
    listed = jnp.zeros((NB, 128), f32)
    for r in range(DONORS):
        count = jnp.zeros((NB, 128), f32)
        for t in range(3):
            count = count + jnp.where(members[r : r + 1, 128 * t : 128 * t + 128] == empties, 1.0, 0.0)
        listed = listed + jnp.dot(count.astype(bf16), hot(lane == POPS + r), preferred_element_type=f32)
    listed_hi = listed.astype(bf16)
    listed_lo = (listed - listed_hi.astype(f32)).astype(bf16)

    listed_both = jnp.concatenate([listed_hi, listed_lo], axis=1)
    pops = jnp.concatenate([pop_hot, jnp.zeros((64, N), bf16)], axis=0)
    folk = jnp.concatenate([jnp.zeros((64, N), bf16), donor_hot, jnp.zeros((48, N), bf16)], axis=0)
    amb_send[15] = jnp.zeros((8, 128), f32)

    native_acc = jnp.zeros((8, N), f32)
    contam_acc = jnp.zeros((8, N), f32)
    totals = jnp.zeros((8, 128), f32)

    x_at, y_at = d // 4, lax.rem(d, 4)

    def to_x(first, count, index):
        copies = []
        for j in (2, 1, 3):
            there = lax.rem(x_at + j, 4)
            copies.append(
                pltpu.make_async_remote_copy(
                    pop_send.at[there, pl.ds(first, count)], x_got.at[j - 1, pl.ds(first, count)],
                    s_sem.at[index], r_sem.at[index], device_id={"donor": 4 * there + y_at}, device_id_type=MESH,
                )
            )
            copies[-1].start()
        return copies

    def look_up(c):
        part = table[:, CHUNK * c : CHUNK * c + CHUNK]
        return lax.dot_general(part, hots[...], FIRST, preferred_element_type=f32)

    for c in x_in + [b_in]:
        c.wait()
    ahead = look_up(0)
    for c in range(5):
        log_odds = ahead
        if c < 4:
            ahead = look_up(c + 1)
        if c < 4:
            counts, blanks = xs[CHUNK * c : CHUNK * c + CHUNK], bs[CHUNK * c : CHUNK * c + CHUNK]
        else:
            counts, blanks = padded_tail(xs), padded_tail(bs)
        half = counts.astype(f32) * 0.5
        swing = half * jnp.tanh(log_odds)
        native = (half + swing).astype(bf16)
        contam = (half - swing).astype(bf16)
        native_acc = native_acc + jnp.sum(native.astype(f32).reshape(CHUNK // 8, 8, N), axis=0)
        contam_acc = contam_acc + jnp.sum(contam.astype(f32).reshape(CHUNK // 8, 8, N), axis=0)
        sums = lax.dot_general(native, pops, LAST, preferred_element_type=f32)
        sums = sums + lax.dot_general(contam, folk, LAST, preferred_element_type=f32)
        extra = jnp.dot(blanks, listed_both, preferred_element_type=f32)
        sums = sums + (extra[:, 0:128] + extra[:, 128:256])
        totals = totals + jnp.sum(sums.reshape(CHUNK // 8, 8, 128), axis=0)
        for h in range(2):
            t = 2 * c + h
            turned = sums[128 * h : 128 * h + 128].T
            for i in range(16):
                pop_send[i // 4, c, i % 4, 4 * h : 4 * h + 4] = turned[4 * i : 4 * i + 4]
            r = 0
            while r < DONORS:
                u = 12 * t + r
                run = min(DONORS - r, 8 - u % 8)
                amb_send[u // 8, u % 8 : u % 8 + run] = turned[64 + r : 64 + r + run]
                r += run

    plane_out[...] = jnp.sum(totals, axis=0, keepdims=True)
    pl.semaphore_wait(barrier, 46)

    def to_plane(i, carry):
        j = far_first(i, 16)
        pltpu.make_async_remote_copy(
            plane_out, plane_in.at[j - 1], s_sem.at[3], r_sem.at[3], device_id=plane_peer(j), device_id_type=MESH
        ).start()
        return carry

    lax.fori_loop(0, 31, to_plane, 0)
    native_row = jnp.sum(native_acc, axis=0, keepdims=True)
    contam_row = jnp.sum(contam_acc, axis=0, keepdims=True)
    for i in range(8):
        mine[0, i : i + 1] = native_row[:, 128 * i : 128 * i + 128]
        mine[1, i : i + 1] = contam_row[:, 128 * i : 128 * i + 128]
    to_core = pltpu.make_async_remote_copy(
        mine.at[1 - core], from_core, s_sem.at[2], r_sem.at[2], device_id=other, device_id_type=MESH
    )
    to_core.start()

    to_x(0, EARLY, 0)
    to_x(EARLY, 5 - EARLY, 5)
    to_core.wait_recv()
    pair_out[...] = mine[core] + from_core[...]
    across = pltpu.make_async_remote_copy(
        pair_out, pair_in, s_sem.at[4], r_sem.at[4], device_id={"gene": q + 2 - 4 * y_hi}, device_id_type=MESH
    )
    across.start()

    def to_owner(j, carry):
        peer = lax.rem(d + j, 16)
        pltpu.make_async_remote_copy(
            amb_send.at[peer], amb_got.at[j - 1], s_sem.at[1], r_sem.at[1],
            device_id={"donor": peer}, device_id_type=MESH,
        ).start()
        return carry

    lax.fori_loop(1, 16, to_owner, 0)

    across.wait_recv()
    z_out[...] = pair_out[...] + pair_in[...]

    def to_z(i, carry):
        j = far_first(i, 8)
        pltpu.make_async_remote_copy(
            z_out, z_in.at[j - 1], s_sem.at[6], r_sem.at[6], device_id=z_peer(j), device_id_type=MESH
        ).start()
        return carry

    lax.fori_loop(0, 15, to_z, 0)

    def wait_for(ref, sem):
        pltpu.make_async_copy(ref, ref, sem).wait()

    wait_for(plane_in, r_sem.at[3])
    tot_out[...] = plane_out[...] + jnp.sum(plane_in[...], axis=0)

    def total_to_z(i, carry):
        j = far_first(i, 8)
        pltpu.make_async_remote_copy(
            tot_out, tot_in.at[j - 1], s_sem.at[8], r_sem.at[8], device_id=z_peer(j), device_id_type=MESH
        ).start()
        return carry

    lax.fori_loop(0, 15, total_to_z, 0)

    wait_for(amb_got, r_sem.at[1])
    amb_all[d] = amb_send[d] + jnp.sum(amb_got[...], axis=0)

    def to_all(j, carry):
        pltpu.make_async_remote_copy(
            amb_all.at[d], amb_all.at[d], s_sem.at[7], r_sem.at[7],
            device_id={"donor": lax.rem(d + j, 16)}, device_id_type=MESH,
        ).start()
        return carry

    lax.fori_loop(1, 16, to_all, 0)

    three = pl.ds(0, 3)
    wait_for(x_got.at[three, pl.ds(0, EARLY)], r_sem.at[0])
    wait_for(x_got.at[three, pl.ds(EARLY, 5 - EARLY)], r_sem.at[5])
    y_send[...] = pop_send[x_at] + jnp.sum(x_got[...], axis=0)
    to_y = []
    for j in (2, 1, 3):
        there = lax.rem(y_at + j, 4)
        to_y.append(
            pltpu.make_async_remote_copy(
                y_send.at[:, there], y_got.at[j - 1], s_sem.at[9], r_sem.at[9],
                device_id={"donor": 4 * x_at + there}, device_id_type=MESH,
            )
        )
        to_y[-1].start()

    wait_for(z_in, r_sem.at[6])
    ours, theirs = z_out[...], z_in[0]
    for j in range(2, 16):
        if j % 2:
            theirs = theirs + z_in[j - 1]
        else:
            ours = ours + z_in[j - 1]
    native_reads = jnp.where(core == 0, ours, theirs)
    contam_reads = jnp.where(core == 0, theirs, ours)
    out_ref[0:8] = (contam_reads + BETA) / (native_reads + contam_reads + 2.0 * BETA)
    out_ref[8:16] = contam_reads / TOTAL

    wait_for(y_got, r_sem.at[9])
    pop_sums = (y_send[:, y_at] + jnp.sum(y_got[...], axis=0)).reshape(40, 128)
    wait_for(amb_all.at[pl.ds(0, 15)], r_sem.at[7])
    ambient = amb_all[...].reshape(128, 128)
    wait_for(tot_in, r_sem.at[8])
    total = tot_out[...] + jnp.sum(tot_in[...], axis=0)

    def column(wanted, count):
        lanes = lax.broadcasted_iota(jnp.int32, (count, 128), 1)
        rows = lax.broadcasted_iota(jnp.int32, (count, 128), 0)
        return jnp.sum(jnp.where(lanes == wanted(rows), total, 0.0), axis=1, keepdims=True) + TOTAL * PSEUDO

    out_ref[16:56] = TOTAL * (pop_sums + PSEUDO) / column(lambda r: 4 * d + r % 4, 40)
    out_ref[56:184] = TOTAL * (ambient + PSEUDO) / column(lambda r: POPS + r % DONORS, 128)

    wait_for(x_got.at[three, pl.ds(0, EARLY)], s_sem.at[0])
    wait_for(x_got.at[three, pl.ds(EARLY, 5 - EARLY)], s_sem.at[5])
    wait_for(amb_got, s_sem.at[1])
    to_core.wait_send()
    wait_for(plane_in, s_sem.at[3])
    across.wait_send()
    wait_for(z_in, s_sem.at[6])
    wait_for(amb_all.at[pl.ds(0, 15)], s_sem.at[7])
    wait_for(tot_in, s_sem.at[8])
    wait_for(y_got, s_sem.at[9])


def finish(raw_ref, prof_ref, amb_ref, theta_ref, reads_ref):
    theta_ref[...] = raw_ref[0:8]
    reads_ref[...] = raw_ref[8:16]
    for t in range(10):
        width = min(128, G - 128 * t)
        prof_ref[:, 128 * t : 128 * t + width] = raw_ref[16 + 4 * t : 20 + 4 * t, 0:width]
        amb_ref[:, 128 * t : 128 * t + width] = raw_ref[56 + 12 * t : 68 + 12 * t, 0:width]


def body(tallies, blanks, labels, people, members, theta, profiles, ambient):
    hbm = pl.BlockSpec(memory_space=pltpu.HBM)
    vmem = pl.BlockSpec(memory_space=pltpu.VMEM)
    v = pltpu.VMEM
    raw = pl.pallas_call(
        kernel,
        out_shape=jax.ShapeDtypeStruct((184, 128), f32),
        in_specs=[hbm] * 8,
        out_specs=vmem,
        scratch_shapes=[
            v((G, N), bf16), v((G, NB), bf16), v((1, N), jnp.int32), v((1, N), jnp.int32),
            v((DONORS, 384), jnp.int32), v((1, N), f32), v((POPS, G), f32), v((DONORS, G), f32),
            v((256, N), bf16), v((256, GP), bf16),
            v((4, 5, 4, 8, 128), f32), v((3, 5, 4, 8, 128), f32), v((5, 4, 8, 128), f32), v((3, 5, 8, 128), f32),
            v((16, 8, 128), f32), v((15, 8, 128), f32), v((16, 8, 128), f32),
            v((2, 8, 128), f32), v((8, 128), f32), v((8, 128), f32), v((8, 128), f32), v((8, 128), f32),
            v((15, 8, 128), f32), v((1, 128), f32), v((31, 1, 128), f32), v((1, 128), f32), v((15, 1, 128), f32),
            pltpu.SemaphoreType.DMA((12,)), pltpu.SemaphoreType.DMA((10,)), pltpu.SemaphoreType.DMA((10,)),
        ],
        compiler_params=pltpu.CompilerParams(
            collective_id=0, has_side_effects=True, vmem_limit_bytes=56 << 20
        ),
    )(
        tallies.T, blanks.T, labels.reshape(1, N), people.reshape(1, N), members, theta.reshape(1, N),
        profiles, ambient,
    )
    profile, new_ambient, new_theta, reads = pl.pallas_call(
        finish,
        out_shape=(
            jax.ShapeDtypeStruct((4, G), f32),
            jax.ShapeDtypeStruct((DONORS, G), f32),
            jax.ShapeDtypeStruct((8, 128), f32),
            jax.ShapeDtypeStruct((8, 128), f32),
        ),
        in_specs=[vmem],
        out_specs=(vmem,) * 4,
    )(raw)
    return profile, new_ambient, new_theta.reshape(N), reads.reshape(N)


def solution(mesh):
    in_specs = (
        P("donor", "gene"), P("donor", "gene"), P("donor"), P("donor"), P(), P("donor"),
        P(None, "gene"), P(None, "gene"),
    )
    out_specs = (P("donor", "gene"), P(None, "gene"), P("donor"), P("donor"))
    return jax.shard_map(body, mesh=mesh, in_specs=in_specs, out_specs=out_specs, check_vma=False)
```

```python
import jax
import jax.numpy as jnp
from jax import lax
from jax.experimental import pallas as pl
from jax.experimental.pallas import tpu as pltpu
from jax.sharding import PartitionSpec as P

TOTAL = 40352
PSEUDO = 0.5
BETA = 10.0
G, N, NB, GP = 1261, 1024, 256, 1280
POPS, DONORS = 64, 12
CHUNK = 256
EARLY = 3
f32, bf16 = jnp.float32, jnp.bfloat16
MESH = pl.DeviceIdType.MESH
LAST = (((1,), (1,)), ((), ()))
FIRST = (((0,), (0,)), ((), ()))


def thirds(v):
    hi = v.astype(bf16)
    rest = v - hi.astype(f32)
    mid = rest.astype(bf16)
    return hi, mid, (rest - mid.astype(f32)).astype(bf16)


def hot(mask):
    return jnp.where(mask, 1.0, 0.0).astype(bf16)


def padded_tail(ref):
    width = ref.shape[1]
    ragged = jnp.concatenate([ref[1248:G].astype(f32), jnp.zeros((3, width), f32)], axis=0)
    return jnp.concatenate([ref[1024:1248], ragged.astype(bf16), jnp.zeros((16, width), bf16)], axis=0)


def kernel(
    x_hbm, b_hbm, lab_hbm, don_hbm, mem_hbm, th_hbm, e_hbm, p_hbm,
    out_ref,
    xs, bs, lab_v, don_v, mem_v, th_v, e_v, p_v, hots, table,
    pop_send, x_got, y_send, y_got, amb_send, amb_got, amb_all, mine, from_core, pair_out, pair_in, z_out, z_in,
    plane_out, plane_in, tot_out, tot_in,
    in_sem, s_sem, r_sem,
):
    d = lax.axis_index("donor")
    q = lax.axis_index("gene")
    core = lax.rem(q, 2)
    other = {"gene": q + 1 - 2 * core}

    smalls = (
        (lab_hbm, lab_v), (don_hbm, don_v), (th_hbm, th_v), (e_hbm, e_v), (p_hbm, p_v), (mem_hbm, mem_v),
    )
    small_in = [pltpu.make_async_copy(a, b, in_sem.at[i]) for i, (a, b) in enumerate(smalls)]
    for c in small_in:
        c.start()
    x_in = pltpu.make_async_copy(x_hbm, xs, in_sem.at[6])
    b_in = pltpu.make_async_copy(b_hbm, bs, in_sem.at[7])
    x_in.start()
    b_in.start()

    barrier = pltpu.get_barrier_semaphore()
    y_hi = lax.rem(q // 2, 2)
    place = 2 * d + y_hi

    def plane_peer(j):
        to = lax.rem(place + j, 32)
        return {"donor": to // 2, "gene": q + 2 * (lax.rem(to, 2) - y_hi)}

    spot = 2 * (q // 4) + core

    def z_peer(j):
        to = lax.rem(spot + j, 16)
        return {"gene": 4 * (to // 2) + 2 * y_hi + lax.rem(to, 2)}

    def far_first(i, middle):
        return middle + (i + 1) // 2 * (1 - 2 * (i % 2))

    def signal_to(peer):
        pl.semaphore_signal(barrier, inc=1, device_id=peer, device_id_type=MESH)

    def greet_z(i, carry):
        signal_to(z_peer(far_first(i, 8)))
        return carry

    def greet_plane(i, carry):
        signal_to(plane_peer(far_first(i, 16)))
        return carry

    for i in range(31):
        greet_plane(i, 0)
    for i in range(15):
        greet_z(i, 0)

    for c in small_in:
        c.wait()
    labels, people, theta = lab_v[...], don_v[...], th_v[...]
    pop_hot = hot(labels == lax.broadcasted_iota(jnp.int32, (POPS, N), 0))
    donor_hot = hot(people == lax.broadcasted_iota(jnp.int32, (16, N), 0))
    for i in range(3):
        hots[64 * i : 64 * i + 64] = pop_hot
        hots[192 + 16 * i : 208 + 16 * i] = donor_hot
    row = lax.broadcasted_iota(jnp.int32, (16, N), 0)
    odds = jnp.zeros((16, N), f32)
    for i, v in enumerate(thirds((jnp.log(theta) - jnp.log(1.0 - theta)) * -0.5)):
        odds = jnp.where(row == i, v.astype(f32), odds)
    hots[240:256] = odds.astype(bf16)
    for i, v in enumerate(thirds(jnp.log(e_v[...]) * 0.5)):
        table[64 * i : 64 * i + 64, 0:G] = v
    log_ambient = jnp.concatenate([jnp.log(p_v[...]) * -0.5, jnp.zeros((4, G), f32)], axis=0)
    for i, v in enumerate(thirds(log_ambient)):
        table[192 + 16 * i : 208 + 16 * i, 0:G] = v
    table[240:256] = hot(lax.broadcasted_iota(jnp.int32, (16, GP), 0) < 3)
    table[0:240, G:GP] = jnp.zeros((240, GP - G), bf16)

    members = mem_v[...] - d * NB
    here = (members >= 0) & (members < NB)
    members = jnp.where(here, members, -1).astype(f32).astype(bf16)
    empties = lax.broadcasted_iota(jnp.int32, (NB, 128), 0).astype(f32).astype(bf16)
    one, none = jnp.ones((NB, 128), bf16), jnp.zeros((NB, 128), bf16)
    lane = lax.broadcasted_iota(jnp.int32, (128, 128), 1)
    listed = jnp.zeros((NB, 128), f32)
    for r in range(DONORS):
        count = none
        for t in range(3):
            count = count + jnp.where(members[r : r + 1, 128 * t : 128 * t + 128] == empties, one, none)
        listed = listed + jnp.dot(count, hot(lane == POPS + r), preferred_element_type=f32)
    listed_hi = listed.astype(bf16)
    listed_lo = (listed - listed_hi.astype(f32)).astype(bf16)

    listed_both = jnp.concatenate([listed_hi, listed_lo], axis=1)
    pops = jnp.concatenate([pop_hot, jnp.zeros((64, N), bf16)], axis=0)
    folk = jnp.concatenate([jnp.zeros((64, N), bf16), donor_hot, jnp.zeros((48, N), bf16)], axis=0)
    amb_send[15] = jnp.zeros((8, 128), f32)

    native_acc = jnp.zeros((8, N), f32)
    contam_acc = jnp.zeros((8, N), f32)
    totals = jnp.zeros((8, 128), f32)

    x_at, y_at = d // 4, lax.rem(d, 4)

    def to_x(first, count, index):
        copies = []
        for j in (2, 1, 3):
            there = lax.rem(x_at + j, 4)
            copies.append(
                pltpu.make_async_remote_copy(
                    pop_send.at[there, pl.ds(first, count)], x_got.at[j - 1, pl.ds(first, count)],
                    s_sem.at[index], r_sem.at[index], device_id={"donor": 4 * there + y_at}, device_id_type=MESH,
                )
            )
            copies[-1].start()
        return copies

    def look_up(c):
        part = table[:, CHUNK * c : CHUNK * c + CHUNK]
        return lax.dot_general(part, hots[...], FIRST, preferred_element_type=f32)

    x_in.wait()
    b_in.wait()
    ahead = look_up(0)
    for c in range(5):
        log_odds = ahead
        if c < 4:
            ahead = look_up(c + 1)
        if c < 4:
            counts, blanks = xs[CHUNK * c : CHUNK * c + CHUNK], bs[CHUNK * c : CHUNK * c + CHUNK]
        else:
            counts, blanks = padded_tail(xs), padded_tail(bs)
        half = counts.astype(f32) * 0.5
        swing = half * jnp.tanh(log_odds)
        native = (half + swing).astype(bf16)
        contam = (half - swing).astype(bf16)
        native_acc = native_acc + jnp.sum(native.astype(f32).reshape(CHUNK // 8, 8, N), axis=0)
        contam_acc = contam_acc + jnp.sum(contam.astype(f32).reshape(CHUNK // 8, 8, N), axis=0)
        sums = lax.dot_general(native, pops, LAST, preferred_element_type=f32)
        sums = sums + lax.dot_general(contam, folk, LAST, preferred_element_type=f32)
        extra = jnp.dot(blanks, listed_both, preferred_element_type=f32)
        sums = sums + (extra[:, 0:128] + extra[:, 128:256])
        totals = totals + jnp.sum(sums.reshape(CHUNK // 8, 8, 128), axis=0)
        for h in range(2):
            t = 2 * c + h
            turned = sums[128 * h : 128 * h + 128].T
            for i in range(16):
                pop_send[i // 4, c, i % 4, 4 * h : 4 * h + 4] = turned[4 * i : 4 * i + 4]
            r = 0
            while r < DONORS:
                u = 12 * t + r
                run = min(DONORS - r, 8 - u % 8)
                amb_send[u // 8, u % 8 : u % 8 + run] = turned[64 + r : 64 + r + run]
                r += run

    plane_out[...] = jnp.sum(totals, axis=0, keepdims=True)
    pl.semaphore_wait(barrier, 46)

    def to_plane(i, carry):
        j = far_first(i, 16)
        pltpu.make_async_remote_copy(
            plane_out, plane_in.at[j - 1], s_sem.at[3], r_sem.at[3], device_id=plane_peer(j), device_id_type=MESH
        ).start()
        return carry

    for i in range(31):
        to_plane(i, 0)
    native_row = jnp.sum(native_acc, axis=0, keepdims=True)
    contam_row = jnp.sum(contam_acc, axis=0, keepdims=True)
    for i in range(8):
        mine[0, i : i + 1] = native_row[:, 128 * i : 128 * i + 128]
        mine[1, i : i + 1] = contam_row[:, 128 * i : 128 * i + 128]
    to_core = pltpu.make_async_remote_copy(
        mine.at[1 - core], from_core, s_sem.at[2], r_sem.at[2], device_id=other, device_id_type=MESH
    )
    to_core.start()

    to_x(0, EARLY, 0)
    to_x(EARLY, 5 - EARLY, 5)
    to_core.wait_recv()
    pair_out[...] = mine[core] + from_core[...]
    across = pltpu.make_async_remote_copy(
        pair_out, pair_in, s_sem.at[4], r_sem.at[4], device_id={"gene": q + 2 - 4 * y_hi}, device_id_type=MESH
    )
    across.start()

    def to_owner(j, carry):
        peer = lax.rem(d + j, 16)
        pltpu.make_async_remote_copy(
            amb_send.at[peer], amb_got.at[j - 1], s_sem.at[1], r_sem.at[1],
            device_id={"donor": peer}, device_id_type=MESH,
        ).start()
        return carry

    lax.fori_loop(1, 16, to_owner, 0)

    across.wait_recv()
    z_out[...] = pair_out[...] + pair_in[...]

    def to_z(i, carry):
        j = far_first(i, 8)
        pltpu.make_async_remote_copy(
            z_out, z_in.at[j - 1], s_sem.at[6], r_sem.at[6], device_id=z_peer(j), device_id_type=MESH
        ).start()
        return carry

    lax.fori_loop(0, 15, to_z, 0)

    def wait_for(ref, sem):
        pltpu.make_async_copy(ref, ref, sem).wait()

    wait_for(plane_in, r_sem.at[3])
    tot_out[...] = plane_out[...] + jnp.sum(plane_in[...], axis=0)

    def total_to_z(i, carry):
        j = far_first(i, 8)
        pltpu.make_async_remote_copy(
            tot_out, tot_in.at[j - 1], s_sem.at[8], r_sem.at[8], device_id=z_peer(j), device_id_type=MESH
        ).start()
        return carry

    for i in range(15):
        total_to_z(i, 0)

    wait_for(amb_got, r_sem.at[1])
    amb_all[d] = amb_send[d] + jnp.sum(amb_got[...], axis=0)

    def to_all(j, carry):
        pltpu.make_async_remote_copy(
            amb_all.at[d], amb_all.at[d], s_sem.at[7], r_sem.at[7],
            device_id={"donor": lax.rem(d + j, 16)}, device_id_type=MESH,
        ).start()
        return carry

    lax.fori_loop(1, 16, to_all, 0)

    three = pl.ds(0, 3)
    wait_for(x_got.at[three, pl.ds(0, EARLY)], r_sem.at[0])
    wait_for(x_got.at[three, pl.ds(EARLY, 5 - EARLY)], r_sem.at[5])
    y_send[...] = pop_send[x_at] + jnp.sum(x_got[...], axis=0)
    to_y = []
    for j in (2, 1, 3):
        there = lax.rem(y_at + j, 4)
        to_y.append(
            pltpu.make_async_remote_copy(
                y_send.at[:, there], y_got.at[j - 1], s_sem.at[9], r_sem.at[9],
                device_id={"donor": 4 * x_at + there}, device_id_type=MESH,
            )
        )
        to_y[-1].start()

    wait_for(z_in, r_sem.at[6])
    ours, theirs = z_out[...], z_in[0]
    for j in range(2, 16):
        if j % 2:
            theirs = theirs + z_in[j - 1]
        else:
            ours = ours + z_in[j - 1]
    native_reads = jnp.where(core == 0, ours, theirs)
    contam_reads = jnp.where(core == 0, theirs, ours)
    out_ref[0:8] = (contam_reads + BETA) / (native_reads + contam_reads + 2.0 * BETA)
    out_ref[8:16] = contam_reads / TOTAL

    wait_for(y_got, r_sem.at[9])
    pop_sums = (y_send[:, y_at] + jnp.sum(y_got[...], axis=0)).reshape(40, 128)
    wait_for(amb_all.at[pl.ds(0, 15)], r_sem.at[7])
    ambient = amb_all[...].reshape(128, 128)
    over_pops = TOTAL * (pop_sums + PSEUDO)
    over_ambient = TOTAL * (ambient + PSEUDO)
    wait_for(x_got.at[three, pl.ds(0, EARLY)], s_sem.at[0])
    wait_for(x_got.at[three, pl.ds(EARLY, 5 - EARLY)], s_sem.at[5])
    wait_for(amb_got, s_sem.at[1])
    to_core.wait_send()
    wait_for(plane_in, s_sem.at[3])
    across.wait_send()
    wait_for(z_in, s_sem.at[6])
    wait_for(amb_all.at[pl.ds(0, 15)], s_sem.at[7])
    wait_for(y_got, s_sem.at[9])
    wait_for(tot_in, r_sem.at[8])
    total = tot_out[...] + jnp.sum(tot_in[...], axis=0)

    def column(wanted, count):
        lanes = lax.broadcasted_iota(jnp.int32, (count, 128), 1)
        rows = lax.broadcasted_iota(jnp.int32, (count, 128), 0)
        return jnp.sum(jnp.where(lanes == wanted(rows), total, 0.0), axis=1, keepdims=True) + TOTAL * PSEUDO

    pop_column = column(lambda r: 4 * d + r % 4, 8)
    out_ref[16:56] = (over_pops.reshape(5, 8, 128) / pop_column[None]).reshape(40, 128)
    ambient_column = column(lambda r: POPS + r % DONORS, 24)
    for k in range(0, 128, 24):
        rows = min(24, 128 - k)
        out_ref[56 + k : 56 + k + rows] = over_ambient[k : k + rows] / ambient_column[0:rows]
    wait_for(tot_in, s_sem.at[8])


def finish(raw_ref, prof_ref, amb_ref, theta_ref, reads_ref):
    theta_ref[...] = raw_ref[0:8]
    reads_ref[...] = raw_ref[8:16]
    for t in range(10):
        width = min(128, G - 128 * t)
        prof_ref[:, 128 * t : 128 * t + width] = raw_ref[16 + 4 * t : 20 + 4 * t, 0:width]
        amb_ref[:, 128 * t : 128 * t + width] = raw_ref[56 + 12 * t : 68 + 12 * t, 0:width]


def body(tallies, blanks, labels, people, members, theta, profiles, ambient):
    hbm = pl.BlockSpec(memory_space=pltpu.HBM)
    vmem = pl.BlockSpec(memory_space=pltpu.VMEM)
    v = pltpu.VMEM
    raw = pl.pallas_call(
        kernel,
        out_shape=jax.ShapeDtypeStruct((184, 128), f32),
        in_specs=[hbm] * 8,
        out_specs=vmem,
        scratch_shapes=[
            v((G, N), bf16), v((G, NB), bf16), v((1, N), jnp.int32), v((1, N), jnp.int32),
            v((DONORS, 384), jnp.int32), v((1, N), f32), v((POPS, G), f32), v((DONORS, G), f32),
            v((256, N), bf16), v((256, GP), bf16),
            v((4, 5, 4, 8, 128), f32), v((3, 5, 4, 8, 128), f32), v((5, 4, 8, 128), f32), v((3, 5, 8, 128), f32),
            v((16, 8, 128), f32), v((15, 8, 128), f32), v((16, 8, 128), f32),
            v((2, 8, 128), f32), v((8, 128), f32), v((8, 128), f32), v((8, 128), f32), v((8, 128), f32),
            v((15, 8, 128), f32), v((1, 128), f32), v((31, 1, 128), f32), v((1, 128), f32), v((15, 1, 128), f32),
            pltpu.SemaphoreType.DMA((8,)), pltpu.SemaphoreType.DMA((10,)), pltpu.SemaphoreType.DMA((10,)),
        ],
        compiler_params=pltpu.CompilerParams(
            collective_id=0, has_side_effects=True, vmem_limit_bytes=56 << 20
        ),
    )(
        tallies.T, blanks.T, labels.reshape(1, N), people.reshape(1, N), members, theta.reshape(1, N),
        profiles, ambient,
    )
    profile, new_ambient, new_theta, reads = pl.pallas_call(
        finish,
        out_shape=(
            jax.ShapeDtypeStruct((4, G), f32),
            jax.ShapeDtypeStruct((DONORS, G), f32),
            jax.ShapeDtypeStruct((8, 128), f32),
            jax.ShapeDtypeStruct((8, 128), f32),
        ),
        in_specs=[vmem],
        out_specs=(vmem,) * 4,
    )(raw)
    return profile, new_ambient, new_theta.reshape(N), reads.reshape(N)


def solution(mesh):
    in_specs = (
        P("donor", "gene"), P("donor", "gene"), P("donor"), P("donor"), P(), P("donor"),
        P(None, "gene"), P(None, "gene"),
    )
    out_specs = (P("donor", "gene"), P(None, "gene"), P("donor"), P("donor"))
    return jax.shard_map(body, mesh=mesh, in_specs=in_specs, out_specs=out_specs, check_vma=False)
```
